32 devices in a mesh: groups: 2 (over y), ctx: 16 (over z, x, core).
Axes of the slice: x: 2, y: 2, z: 4, core: 2. Of those that a mesh axis runs over, the one named last changes fastest.
Arguments:
- inputs: bfloat16 [8192, 1024], P(('groups', 'ctx')), parts along dimension 0, may hold values from -6 to 6
- out_grad: bfloat16 [8192, 1024], P(('groups', 'ctx')), parts along dimension 0, may hold values from -6 to 6
- filter_taps: float32 [2048, 1024], P('groups'), parts along dimension 0, may hold values from -0.1875 to 0.1875
- block_owner: int32 [16], replicated, may hold values from 0 to 15, each once
Outputs:
- input_grad: bfloat16 [8192, 1024], P(('groups', 'ctx')), parts along dimension 0
- filter_grad: float32 [2048, 1024], P(('groups', 'ctx')), parts along dimension 0
The draws below stay inside these ranges and needn't reach their ends.
There are 2 independent parts, one for each index of `groups`. The reference program is written for one: setup_inputs(seed, part) draws one part's arguments, and reference() takes and returns one part's arrays. A program takes and returns all parts, laid end to end along the dimension named above; an argument that names none is the same for every part. Nothing has to cross between parts.
Inputs may be any that keep to these rules, and one draw needn't show every extreme that they name: block_owner names every ctx index exactly once.
All inputs are finite; a program needn't handle non-finite values.
Results may differ from the reference program's by a relative error of at most 0.007.
Values may be sent and summed in bfloat16 or wider, within the bound.
A program may use at most 128 MiB of HBM per device.

```python
import math
import jax
import jax.numpy as jnp

CH = 1024
LAGS = 1024
TOKENS = 4096
OWNERS = 16
LAG_BLOCK = 64


def steps_of(rng, extent, shards, smallest, top_value):
    loudness = 1.0
    for axis_at, parts in shards:
        heights = jax.random.uniform(jax.random.fold_in(jax.random.fold_in(rng, 6), axis_at), (parts,), jnp.float32, smallest / len(shards), top_value / len(shards))
        loudness = loudness * jnp.repeat(jnp.exp(heights), extent[axis_at] // parts).reshape((-1,) + (1,) * (len(extent) - 1 - axis_at))
    return loudness


def gaussian(own_key, extent, spread, reach, cuts=(), held_as=jnp.bfloat16):
    result = jax.random.normal(own_key, extent, jnp.float32) * spread
    if len(cuts) > 0:
        result = steps_of(own_key, extent, cuts, -0.22, 0.18) * result
    return jnp.clip(result, min=-reach, max=reach).astype(held_as)


def setup_inputs(seed: int = 0, part: int = 0) -> dict:
    arg_keys = jax.random.split(jax.random.key(seed), 5)
    part_splits = jax.random.split(jax.random.fold_in(arg_keys[4], part), 5)
    inputs = gaussian(part_splits[0], (TOKENS, CH), 1.0, 6.0, ((0, 16),))
    out_grad = gaussian(part_splits[1], (TOKENS, CH), 1.0, 6.0, ((0, 16),))
    filter_taps = gaussian(part_splits[2], (LAGS, CH), LAGS ** -0.5, 0.1875, (), jnp.float32)
    block_owner = jax.random.permutation(arg_keys[3], OWNERS).astype(jnp.int32)
    return {"inputs": inputs, "out_grad": out_grad, "filter_taps": filter_taps, "block_owner": block_owner}


def reference(inputs, out_grad, filter_taps, block_owner):
    signal = inputs.astype(jnp.float32)
    cotangent = out_grad.astype(jnp.float32)
    taps = filter_taps.astype(jnp.float32)
    span = 1 << (TOKENS + LAGS - 1).bit_length()
    grad_freq = jnp.fft.rfft(cotangent, n=span, axis=0)
    taps_freq = jnp.fft.rfft(taps, n=span, axis=0)
    input_grad = jnp.fft.irfft(jnp.conj(taps_freq) * grad_freq, n=span, axis=0)[:TOKENS]
    signal_freq = jnp.fft.rfft(signal, n=span, axis=0)
    lag_grad = jnp.fft.irfft(jnp.conj(signal_freq) * grad_freq, n=span, axis=0)[:LAGS]
    holder = jnp.zeros((OWNERS,), jnp.int32).at[block_owner].set(jnp.arange(OWNERS, dtype=jnp.int32))
    ordered = jnp.take(lag_grad.reshape(OWNERS, LAG_BLOCK, CH), holder, axis=0).reshape(LAGS, CH)
    filter_grad = ordered * (1.0 / math.sqrt(TOKENS))
    return (input_grad.astype(jnp.float32).astype(jnp.bfloat16), filter_grad.astype(jnp.float32))
```

```python
import functools
import math

import jax
import jax.numpy as jnp
import ml_dtypes
import numpy as np
from jax import lax
from jax.experimental import pallas as pl
from jax.experimental.pallas import tpu as pltpu
from jax.sharding import PartitionSpec as P

MESH = pl.DeviceIdType.MESH
ROWS = 16
LANES = 128


def make_tables(block):
    order = np.concatenate([np.arange(0, block, 2), np.arange(1, block, 2)]).astype(np.int64)
    place = np.arange(block, dtype=np.int64)
    period = 4 * block
    ahead = ((2 * order + 1)[:, None] * place[None, :]) % period
    ahead = ahead * (2.0 * math.pi / period)
    forward = np.concatenate([np.cos(ahead), -np.sin(ahead)], axis=0)
    inverse = np.concatenate([np.cos(ahead), -np.sin(ahead)], axis=0).T / block
    behind = ((2 * order + 1)[:, None] * (block - place)[None, :]) % period
    behind = behind * (2.0 * math.pi / period)
    backward = np.concatenate([np.cos(behind), -np.sin(behind)], axis=0).T / block
    return [t.astype(np.float32).astype(ml_dtypes.bfloat16) for t in (forward, inverse, backward)]


def kernel(
    gang,
    planes,
    scale,
    holder_ref,
    fwd_ref,
    inv_ref,
    back_ref,
    x_ref,
    g_ref,
    taps_ref,
    o_ref,
    f_ref,
    xbuf,
    gbuf,
    taps,
    xspec,
    gspec,
    fspec,
    prod,
    lag,
    outbuf,
    lag_send,
    lag_recv,
    lag_sum,
    local_sem,
    x_send,
    x_recv,
    g_send,
    g_recv,
    xh_send,
    xh_recv,
    gh_send,
    gh_recv,
    o_send,
    o_recv,
    l_send,
    l_recv,
    f_send,
    f_recv,
):
    me = lax.axis_index("ctx")
    q = me // gang
    j = me % gang
    block, width = xbuf.shape[2], xbuf.shape[3]
    lag_block = f_ref.shape[0]
    half = block // 2

    def peer(d):
        found = 0
        bit = 1
        while bit < gang:
            found = found + ((j // bit + d // bit) % 2) * bit
            bit *= 2
        return found

    def cols(at):
        return pl.ds(pl.multiple_of(at * width, width), width)

    def remote(src, dst, send, recv, plane, at):
        return pltpu.make_async_remote_copy(
            src_ref=src,
            dst_ref=dst,
            send_sem=send,
            recv_sem=recv,
            device_id={"ctx": plane * gang + at},
            device_id_type=MESH,
        )

    own_x = pltpu.make_async_copy(x_ref.at[:, cols(j)], xbuf.at[1, j], local_sem.at[0])
    own_g = pltpu.make_async_copy(g_ref.at[:, cols(j)], gbuf.at[0, j], local_sem.at[1])
    own_taps = pltpu.make_async_copy(taps_ref.at[:, cols(j)], taps, local_sem.at[2])
    own_x.start()
    own_g.start()
    own_taps.start()

    barrier = pltpu.get_barrier_semaphore()
    for d in range(1, gang):
        pl.semaphore_signal(
            barrier, inc=1, device_id={"ctx": q * gang + peer(d)}, device_id_type=MESH
        )
    for e in range(1, planes):
        pl.semaphore_signal(
            barrier, inc=1, device_id={"ctx": ((q + e) % planes) * gang + j}, device_id_type=MESH
        )
    pl.semaphore_wait(barrier, gang - 1 + planes - 1)

    def x_copy(d):
        return remote(
            x_ref.at[:, cols(peer(d))], xbuf.at[1, j], x_send.at[d], x_recv.at[d], q, peer(d)
        )

    def g_copy(d):
        return remote(
            g_ref.at[:, cols(peer(d))], gbuf.at[0, j], g_send.at[d], g_recv.at[d], q, peer(d)
        )

    def x_ahead(d):
        source = x_ref.at[:, cols(j)] if d == 0 else xbuf.at[1, peer(d)]
        return remote(
            source, xbuf.at[0, peer(d)], xh_send.at[d], xh_recv.at[d], (q + 1) % planes, j
        )

    def g_ahead(d):
        source = g_ref.at[:, cols(j)] if d == 0 else gbuf.at[0, peer(d)]
        return remote(
            source,
            gbuf.at[1, peer(d)],
            gh_send.at[d],
            gh_recv.at[d],
            (q + planes - 1) % planes,
            j,
        )

    def arrived(ref, sem, at):
        remote(ref, ref, sem, sem, q, at).wait_recv()

    for d in reversed(range(1, gang)):
        x_copy(d).start()
        g_copy(d).start()

    @pl.when(q + 1 < planes)
    def _():
        x_ahead(0).start()

    @pl.when(q > 0)
    def _():
        g_ahead(0).start()

    @pl.when(q == 0)
    def _():
        xbuf[0] = jnp.zeros(xbuf.shape[1:], xbuf.dtype)

    @pl.when(q == planes - 1)
    def _():
        gbuf[1] = jnp.zeros(gbuf.shape[1:], gbuf.dtype)

    def spectrum(value):
        return jnp.dot(fwd_ref[...], value, preferred_element_type=jnp.float32)

    for d in range(1, gang):
        arrived(xbuf.at[1, peer(d)], x_recv.at[d], peer(d))

        @pl.when(q + 1 < planes)
        def _():
            x_ahead(d).start()

        arrived(gbuf.at[0, peer(d)], g_recv.at[d], peer(d))

        @pl.when(q > 0)
        def _():
            g_ahead(d).start()

    own_taps.wait()

    @pl.loop(0, gang)
    def _(t):
        rows = pl.ds(pl.multiple_of(t * block, block), block)
        fspec[t] = spectrum(taps[rows, :].astype(jnp.bfloat16))

    own_x.wait()
    own_g.wait()

    @pl.loop(0, gang)
    def _(t):
        xspec[gang + t] = spectrum(xbuf[1, t])
        gspec[t] = spectrum(gbuf[0, t])

    @pl.when(q > 0)
    def _():
        for d in range(gang):
            arrived(xbuf.at[0, peer(d)], xh_recv.at[d], j)

    @pl.loop(0, gang)
    def _(t):
        xspec[t] = spectrum(xbuf[0, t])

    def tiles(body):
        for part, sign in ((0, 1.0), (1, -1.0)):
            for lane in range(width // LANES):

                @pl.loop(0, half // ROWS)
                def _(step):
                    first = pl.multiple_of(part * half + step * ROWS, ROWS)
                    second = pl.multiple_of(block + part * half + step * ROWS, ROWS)
                    at = pl.ds(lane * LANES, LANES)
                    body(pl.ds(first, ROWS), pl.ds(second, ROWS), at, sign)

    def windows(spec, real, imag, at, sign):
        parts = [(spec[w, real, at], spec[w, imag, at]) for w in range(2 * gang)]
        found = []
        for w in range(2 * gang - 1):
            low, high = parts[w], parts[w + 1]
            if sign > 0:
                found.append((low[0] + high[1], low[1] - high[0]))
            else:
                found.append((low[0] - high[1], low[1] + high[0]))
        return found

    def lag_tile(real, imag, at, sign):
        window = windows(xspec, real, imag, at, sign)
        own = [(gspec[t, real, at], gspec[t, imag, at]) for t in range(gang)]
        for o in range(gang):
            total_r, total_i = None, None
            for t in range(gang):
                a, b = own[t], window[gang + t - o - 1]
                r = a[0] * b[0] + a[1] * b[1]
                i = a[0] * b[1] - a[1] * b[0]
                total_r = r if total_r is None else total_r + r
                total_i = i if total_i is None else total_i + i
            prod[o, real, at] = total_r.astype(jnp.bfloat16)
            prod[o, imag, at] = total_i.astype(jnp.bfloat16)

    tiles(lag_tile)

    @pl.loop(0, gang)
    def _(o):
        found = jnp.dot(back_ref[...], prod[o], preferred_element_type=jnp.float32)
        count = block // lag_block
        lag[pl.ds(o * count, count)] = found.reshape(count, lag_block, width)

    def lag_copy(e):
        to = (q + e) % planes
        return remote(lag_send.at[to], lag_recv.at[q], l_send.at[e], l_recv.at[e], to, j)

    for e in range(planes):
        to = (q + e + 1) % planes
        pieces = []
        for at in range(gang):
            pieces.append(lag[holder_ref[to * gang + at]])
        whole = jnp.concatenate(pieces, axis=0)
        if e < planes - 1:
            lag_send[to] = whole.astype(jnp.bfloat16)
            lag_copy(e + 1).start()
        else:
            lag_sum[...] = whole

    @pl.when(q < planes - 1)
    def _():
        for d in range(gang):
            arrived(gbuf.at[1, peer(d)], gh_recv.at[d], j)

    @pl.loop(0, gang)
    def _(t):
        gspec[gang + t] = spectrum(gbuf[1, t])

    def grad_tile(real, imag, at, sign):
        window = windows(gspec, real, imag, at, sign)
        own = [(fspec[o, real, at], fspec[o, imag, at]) for o in range(gang)]
        for t in range(gang):
            total_r, total_i = None, None
            for o in range(gang):
                a, b = own[o], window[t + o]
                r = a[0] * b[0] + a[1] * b[1]
                i = a[0] * b[1] - a[1] * b[0]
                total_r = r if total_r is None else total_r + r
                total_i = i if total_i is None else total_i + i
            prod[t, real, at] = total_r.astype(jnp.bfloat16)
            prod[t, imag, at] = total_i.astype(jnp.bfloat16)

    tiles(grad_tile)

    def o_copy(d):
        return remote(
            outbuf.at[peer(d)], o_ref.at[:, cols(j)], o_send.at[d], o_recv.at[d], q, peer(d)
        )

    own_o = pltpu.make_async_copy(outbuf.at[j], o_ref.at[:, cols(j)], local_sem.at[3])
    for d in list(range(gang - 1, 0, -1)) + [0]:
        at = peer(d)
        outbuf[at] = jnp.dot(inv_ref[...], prod[at], preferred_element_type=jnp.float32).astype(
            jnp.bfloat16
        )
        if d > 0:
            o_copy(d).start()
        else:
            own_o.start()

    for e in range(1, planes):
        source = (q + planes - e) % planes
        remote(
            lag_recv.at[source], lag_recv.at[source], l_recv.at[e], l_recv.at[e], source, j
        ).wait_recv()
        lag_sum[...] = lag_sum[...] + lag_recv[source].astype(jnp.float32)
    lag_sum[...] = lag_sum[...] * scale

    def lag_rows(at):
        return lag_sum.at[pl.ds(pl.multiple_of(at * lag_block, lag_block), lag_block), :]

    def f_copy(d):
        return remote(
            lag_rows(peer(d)), f_ref.at[:, cols(j)], f_send.at[d], f_recv.at[d], q, peer(d)
        )

    own_f = pltpu.make_async_copy(lag_rows(j), f_ref.at[:, cols(j)], local_sem.at[4])
    for d in reversed(range(1, gang)):
        f_copy(d).start()
    own_f.start()

    for d in range(1, gang):
        arrived(o_ref.at[:, cols(peer(d))], o_recv.at[d], peer(d))
        arrived(f_ref.at[:, cols(peer(d))], f_recv.at[d], peer(d))
        x_copy(d).wait_send()
        g_copy(d).wait_send()
        o_copy(d).wait_send()
        f_copy(d).wait_send()
    for e in range(1, planes):
        lag_copy(e).wait_send()

    @pl.when(q + 1 < planes)
    def _():
        for d in range(gang):
            x_ahead(d).wait_send()

    @pl.when(q > 0)
    def _():
        for d in range(gang):
            g_ahead(d).wait_send()

    own_o.wait()
    own_f.wait()


def shards(inputs, out_grad, filter_taps, block_owner):
    block, channels = inputs.shape
    devices = lax.axis_size("ctx")
    lags = filter_taps.shape[0]
    gang = lags // block
    planes = devices // gang
    width = channels // gang
    lag_block = lags // devices
    scale = 1.0 / math.sqrt(devices * block)
    ids = jnp.arange(devices, dtype=jnp.int32)
    holder = jnp.sum(
        jnp.where(block_owner[None, :] == ids[:, None], ids[None, :], 0), axis=1, dtype=jnp.int32
    )
    forward, inverse, backward = [jnp.asarray(t) for t in make_tables(block)]
    vmem = pl.BlockSpec(memory_space=pltpu.VMEM)
    hbm = pl.BlockSpec(memory_space=pl.ANY)
    dma = pltpu.SemaphoreType.DMA
    return pl.pallas_call(
        functools.partial(kernel, gang, planes, scale),
        out_shape=(
            jax.ShapeDtypeStruct((block, channels), jnp.bfloat16),
            jax.ShapeDtypeStruct((lag_block, channels), jnp.float32),
        ),
        in_specs=[pl.BlockSpec(memory_space=pltpu.SMEM)] + [vmem] * 3 + [hbm] * 3,
        out_specs=(hbm, hbm),
        scratch_shapes=[
            pltpu.VMEM((2, gang, block, width), jnp.bfloat16),
            pltpu.VMEM((2, gang, block, width), jnp.bfloat16),
            pltpu.VMEM((lags, width), jnp.float32),
            pltpu.VMEM((2 * gang, 2 * block, width), jnp.float32),
            pltpu.VMEM((2 * gang, 2 * block, width), jnp.float32),
            pltpu.VMEM((gang, 2 * block, width), jnp.float32),
            pltpu.VMEM((gang, 2 * block, width), jnp.bfloat16),
            pltpu.VMEM((devices, lag_block, width), jnp.float32),
            pltpu.VMEM((gang, block, width), jnp.bfloat16),
            pltpu.VMEM((planes, gang * lag_block, width), jnp.bfloat16),
            pltpu.VMEM((planes, gang * lag_block, width), jnp.bfloat16),
            pltpu.VMEM((gang * lag_block, width), jnp.float32),
            dma((5,)),
        ]
        + [dma((gang,))] * 10
        + [dma((planes,))] * 2
        + [dma((gang,))] * 2,
        compiler_params=pltpu.CompilerParams(
            collective_id=0, has_side_effects=True, vmem_limit_bytes=44 * 1024 * 1024
        ),
    )(holder, forward, inverse, backward, inputs, out_grad, filter_taps)


def solution(mesh):
    placed = (P(("groups", "ctx"), None), P(("groups", "ctx"), None), P("groups", None), P())
    return jax.shard_map(
        shards,
        mesh=mesh,
        in_specs=placed,
        out_specs=(P(("groups", "ctx"), None), P(("groups", "ctx"), None)),
        check_vma=False,
    )
```

```python
import functools
import math

import jax
import jax.numpy as jnp
import ml_dtypes
import numpy as np
from jax import lax
from jax.experimental import pallas as pl
from jax.experimental.pallas import tpu as pltpu
from jax.sharding import PartitionSpec as P

MESH = pl.DeviceIdType.MESH
ROWS = 16
HALVES = 2
LANES = 128


def make_tables(block):
    order = np.concatenate([np.arange(0, block, 2), np.arange(1, block, 2)]).astype(np.int64)
    place = np.arange(block, dtype=np.int64)
    period = 4 * block
    ahead = ((2 * order + 1)[:, None] * place[None, :]) % period
    ahead = ahead * (2.0 * math.pi / period)
    forward = np.concatenate([np.cos(ahead), -np.sin(ahead)], axis=0)
    inverse = np.concatenate([np.cos(ahead), -np.sin(ahead)], axis=0).T / block
    return [t.astype(np.float32).astype(ml_dtypes.bfloat16) for t in (forward, inverse)]


def kernel(
    gang,
    planes,
    scale,
    holder_ref,
    fwd_hbm,
    inv_hbm,
    x_ref,
    g_ref,
    taps_ref,
    o_ref,
    f_ref,
    fwd_ref,
    inv_ref,
    xbuf,
    gbuf,
    taps,
    xspec,
    gspec,
    fspec,
    prod,
    lag,
    outbuf,
    lag_send,
    lag_recv,
    lag_sum,
    local_sem,
    own_sem,
    x_send,
    x_recv,
    g_send,
    g_recv,
    gh_send,
    gh_recv,
    o_send,
    o_recv,
    f_send,
    f_recv,
    l_send,
    l_recv,
):
    me = lax.axis_index("ctx")
    q = me // gang
    j = me % gang
    halves, block, width = xbuf.shape[0], xbuf.shape[2], xbuf.shape[3]
    lag_block = f_ref.shape[0]
    half = block // 2

    def peer(d):
        found = 0
        bit = 1
        while bit < gang:
            found = found + ((j // bit + d // bit) % 2) * bit
            bit *= 2
        return found

    def cols(at, h):
        return pl.ds(pl.multiple_of((at * halves + h) * width, width), width)

    def remote(src, dst, send, recv, plane, at):
        return pltpu.make_async_remote_copy(
            src_ref=src,
            dst_ref=dst,
            send_sem=send,
            recv_sem=recv,
            device_id={"ctx": plane * gang + at},
            device_id_type=MESH,
        )

    barrier = pltpu.get_barrier_semaphore()
    for d in range(1, gang):
        pl.semaphore_signal(
            barrier, inc=1, device_id={"ctx": q * gang + peer(d)}, device_id_type=MESH
        )
    for e in range(1, planes):
        pl.semaphore_signal(
            barrier, inc=1, device_id={"ctx": ((q + e) % planes) * gang + j}, device_id_type=MESH
        )

    def own(n, h):
        source, target = [
            (x_ref.at[:, cols(j, h)], xbuf.at[h, j]),
            (g_ref.at[:, cols(j, h)], gbuf.at[h, 0, j]),
            (taps_ref.at[:, cols(j, h)], taps.at[h]),
        ][n]
        return pltpu.make_async_copy(source, target, own_sem.at[n, h])

    fetched = [
        pltpu.make_async_copy(fwd_hbm, fwd_ref, local_sem.at[0]),
        pltpu.make_async_copy(inv_hbm, inv_ref, local_sem.at[1]),
    ]
    fetched[0].start()
    for n in (2, 1, 0):
        for h in range(halves):
            own(n, h).start()
    fetched[1].start()

    pl.semaphore_wait(barrier, gang - 1 + planes - 1)

    def x_copy(h, d):
        return remote(
            x_ref.at[:, cols(peer(d), h)],
            xbuf.at[h, j],
            x_send.at[h, d],
            x_recv.at[h, d],
            q,
            peer(d),
        )

    def g_copy(h, d):
        return remote(
            g_ref.at[:, cols(peer(d), h)],
            gbuf.at[h, 0, j],
            g_send.at[h, d],
            g_recv.at[h, d],
            q,
            peer(d),
        )

    def g_ahead(h, d):
        source = g_ref.at[:, cols(j, h)] if d == 0 else gbuf.at[h, 0, peer(d)]
        return remote(
            source,
            gbuf.at[h, 1, peer(d)],
            gh_send.at[h, d],
            gh_recv.at[h, d],
            (q + planes - 1) % planes,
            j,
        )

    def arrived(ref, sem, at):
        remote(ref, ref, sem, sem, q, at).wait_recv()

    far_first = list(range(gang - 1, 0, -1))

    def send_g(h):
        for d in far_first:
            g_copy(h, d).start()

    def send_x(h):
        for d in far_first:
            x_copy(h, d).start()

    send_g(0)
    send_x(0)
    for h in range(halves):

        @pl.when(q > 0)
        def _():
            g_ahead(h, 0).start()

    @pl.when(q == planes - 1)
    def _():
        for h in range(halves):
            gbuf[h, 1] = jnp.zeros(gbuf.shape[2:], gbuf.dtype)

    def spectrum(value):
        return jnp.dot(fwd_ref[...], value, preferred_element_type=jnp.float32)

    fetched[0].wait()

    for h in range(halves):
        own(2, h).wait()

        @pl.loop(0, gang)
        def _(t):
            rows = pl.ds(pl.multiple_of(t * block, block), block)
            fspec[h, t] = spectrum(taps[h, rows, :].astype(jnp.bfloat16))

    def g_arrive(h):
        for d in range(1, gang):
            arrived(gbuf.at[h, 0, peer(d)], g_recv.at[h, d], peer(d))

            @pl.when(q > 0)
            def _():
                g_ahead(h, d).start()

    def x_arrive(h):
        for d in range(1, gang):
            arrived(xbuf.at[h, peer(d)], x_recv.at[h, d], peer(d))

    def g_spectra(h, side):
        @pl.loop(0, gang)
        def _(t):
            gspec[h, side * gang + t] = spectrum(gbuf[h, side, t])

    def x_spectra(h):
        @pl.loop(0, gang)
        def _(t):
            xspec[h, t] = spectrum(xbuf[h, t])

    def tiles(body):
        for part, sign in ((0, 1.0), (1, -1.0)):
            for lane in range(width // LANES):

                @pl.loop(0, half // ROWS)
                def _(step):
                    first = pl.multiple_of(part * half + step * ROWS, ROWS)
                    second = pl.multiple_of(block + part * half + step * ROWS, ROWS)
                    at = pl.ds(lane * LANES, LANES)
                    body(pl.ds(first, ROWS), pl.ds(second, ROWS), at, sign)

    def windows(h, real, imag, at, sign):
        parts = [(gspec[h, w, real, at], gspec[h, w, imag, at]) for w in range(2 * gang)]
        found = []
        for w in range(2 * gang - 1):
            low, high = parts[w], parts[w + 1]
            if sign > 0:
                found.append((low[0] + high[1], low[1] - high[0]))
            else:
                found.append((low[0] - high[1], low[1] + high[0]))
        return found

    def products(spec, h):
        def body(real, imag, at, sign):
            window = windows(h, real, imag, at, sign)
            lone = [(spec[h, t, real, at], spec[h, t, imag, at]) for t in range(gang)]
            for n in range(gang):
                total_r, total_i = None, None
                for t in range(gang):
                    a, b = lone[t], window[n + t]
                    r = a[0] * b[0] + a[1] * b[1]
                    i = a[0] * b[1] - a[1] * b[0]
                    total_r = r if total_r is None else total_r + r
                    total_i = i if total_i is None else total_i + i
                prod[n, real, at] = total_r.astype(jnp.bfloat16)
                prod[n, imag, at] = total_i.astype(jnp.bfloat16)

        tiles(body)

    def lag_copy(h, e):
        to = (q + e) % planes
        return remote(
            lag_send.at[h, to], lag_recv.at[h, q], l_send.at[h, e], l_recv.at[h, e], to, j
        )

    def lag_part(h):
        @pl.when(q < planes - 1)
        def _():
            for d in range(gang):
                arrived(gbuf.at[h, 1, peer(d)], gh_recv.at[h, d], j)

        g_spectra(h, 1)
        products(xspec, h)

        @pl.loop(0, gang)
        def _(o):
            found = jnp.dot(inv_ref[...], prod[o], preferred_element_type=jnp.float32)
            count = block // lag_block
            lag[pl.ds(o * count, count)] = found.reshape(count, lag_block, width)

        for e in range(planes):
            to = (q + e + 1) % planes
            pieces = []
            for at in range(gang):
                pieces.append(lag[holder_ref[to * gang + at]])
            whole = jnp.concatenate(pieces, axis=0)
            if e < planes - 1:
                lag_send[h, to] = whole.astype(jnp.bfloat16)
                lag_copy(h, e + 1).start()
            else:
                lag_sum[h] = whole

    def o_copy(h, d):
        return remote(
            outbuf.at[h, peer(d)],
            o_ref.at[:, cols(j, h)],
            o_send.at[h, d],
            o_recv.at[h, d],
            q,
            peer(d),
        )

    def own_o(h):
        return pltpu.make_async_copy(outbuf.at[h, j], o_ref.at[:, cols(j, h)], own_sem.at[3, h])

    def grad_part(h):
        products(fspec, h)

        @pl.loop(0, gang)
        def _(t):
            outbuf[h, t] = jnp.dot(
                inv_ref[...], prod[t], preferred_element_type=jnp.float32
            ).astype(jnp.bfloat16)

    def send_o(h):
        for d in far_first:
            o_copy(h, d).start()
        own_o(h).start()

    def lag_rows(h, at):
        return lag_sum.at[h, pl.ds(pl.multiple_of(at * lag_block, lag_block), lag_block), :]

    def f_copy(h, d):
        return remote(
            lag_rows(h, peer(d)),
            f_ref.at[:, cols(j, h)],
            f_send.at[h, d],
            f_recv.at[h, d],
            q,
            peer(d),
        )

    def own_f(h):
        return pltpu.make_async_copy(lag_rows(h, j), f_ref.at[:, cols(j, h)], own_sem.at[4, h])

    def lag_finish(h):
        total = lag_sum[h]
        for e in range(1, planes):
            source = (q + planes - e) % planes
            arrived(lag_recv.at[h, source], l_recv.at[h, e], j)
            total = total + lag_recv[h, source].astype(jnp.float32)
        lag_sum[h] = total * scale
        for d in far_first:
            f_copy(h, d).start()
        own_f(h).start()

    for h in range(halves):
        g_arrive(h)
        if h + 1 < halves:
            send_g(h + 1)
        own(1, h).wait()
        g_spectra(h, 0)
        if h == 0:
            fetched[1].wait()
        else:
            grad_part(h - 1)
        x_arrive(h)
        if h + 1 < halves:
            send_x(h + 1)
        own(0, h).wait()
        x_spectra(h)
        if h > 0:
            send_o(h - 1)
        lag_part(h)
    grad_part(halves - 1)
    send_o(halves - 1)
    for h in range(halves):
        lag_finish(h)

    for h in range(halves):
        for d in range(1, gang):
            arrived(o_ref.at[:, cols(peer(d), h)], o_recv.at[h, d], peer(d))
            arrived(f_ref.at[:, cols(peer(d), h)], f_recv.at[h, d], peer(d))
            x_copy(h, d).wait_send()
            g_copy(h, d).wait_send()
            o_copy(h, d).wait_send()
            f_copy(h, d).wait_send()
        for e in range(1, planes):
            lag_copy(h, e).wait_send()

        @pl.when(q > 0)
        def _():
            for d in range(gang):
                g_ahead(h, d).wait_send()

        own_o(h).wait()
        own_f(h).wait()


def shards(inputs, out_grad, filter_taps, block_owner):
    block, channels = inputs.shape
    devices = lax.axis_size("ctx")
    lags = filter_taps.shape[0]
    gang = lags // block
    planes = devices // gang
    width = channels // gang // HALVES
    lag_block = lags // devices
    scale = 1.0 / math.sqrt(devices * block)
    ids = jnp.arange(devices, dtype=jnp.int32)
    holder = jnp.sum(
        jnp.where(block_owner[None, :] == ids[:, None], ids[None, :], 0), axis=1, dtype=jnp.int32
    )
    forward, inverse = [jnp.asarray(t) for t in make_tables(block)]
    hbm = pl.BlockSpec(memory_space=pltpu.HBM)
    dma = pltpu.SemaphoreType.DMA
    return pl.pallas_call(
        functools.partial(kernel, gang, planes, scale),
        out_shape=(
            jax.ShapeDtypeStruct((block, channels), jnp.bfloat16),
            jax.ShapeDtypeStruct((lag_block, channels), jnp.float32),
        ),
        in_specs=[pl.BlockSpec(memory_space=pltpu.SMEM)] + [hbm] * 5,
        out_specs=(hbm, hbm),
        scratch_shapes=[
            pltpu.VMEM(forward.shape, jnp.bfloat16),
            pltpu.VMEM(inverse.shape, jnp.bfloat16),
            pltpu.VMEM((HALVES, gang, block, width), jnp.bfloat16),
            pltpu.VMEM((HALVES, 2, gang, block, width), jnp.bfloat16),
            pltpu.VMEM((HALVES, lags, width), jnp.float32),
            pltpu.VMEM((HALVES, gang, 2 * block, width), jnp.float32),
            pltpu.VMEM((HALVES, 2 * gang, 2 * block, width), jnp.float32),
            pltpu.VMEM((HALVES, gang, 2 * block, width), jnp.float32),
            pltpu.VMEM((gang, 2 * block, width), jnp.bfloat16),
            pltpu.VMEM((devices, lag_block, width), jnp.float32),
            pltpu.VMEM((HALVES, gang, block, width), jnp.bfloat16),
            pltpu.VMEM((HALVES, planes, gang * lag_block, width), jnp.bfloat16),
            pltpu.VMEM((HALVES, planes, gang * lag_block, width), jnp.bfloat16),
            pltpu.VMEM((HALVES, gang * lag_block, width), jnp.float32),
            dma((2,)),
            dma((5, HALVES)),
        ]
        + [dma((HALVES, gang))] * 10
        + [dma((HALVES, planes))] * 2,
        compiler_params=pltpu.CompilerParams(
            collective_id=0, has_side_effects=True, vmem_limit_bytes=62 * 1024 * 1024
        ),
    )(holder, forward, inverse, inputs, out_grad, filter_taps)


def solution(mesh):
    placed = (P(("groups", "ctx"), None), P(("groups", "ctx"), None), P("groups", None), P())
    return jax.shard_map(
        shards,
        mesh=mesh,
        in_specs=placed,
        out_specs=(P(("groups", "ctx"), None), P(("groups", "ctx"), None)),
        check_vma=False,
    )
```

```python
import functools
import math

import jax
import jax.numpy as jnp
import ml_dtypes
import numpy as np
from jax import lax
from jax.experimental import pallas as pl
from jax.experimental.pallas import tpu as pltpu
from jax.sharding import PartitionSpec as P

MESH = pl.DeviceIdType.MESH
ROWS = 16
HALVES = 2
LANES = 128


def make_tables(block):
    order = np.concatenate([np.arange(0, block, 2), np.arange(1, block, 2)]).astype(np.int64)
    place = np.arange(block, dtype=np.int64)
    period = 4 * block
    ahead = ((2 * order + 1)[:, None] * place[None, :]) % period
    ahead = ahead * (2.0 * math.pi / period)
    forward = np.concatenate([np.cos(ahead), -np.sin(ahead)], axis=0)
    inverse = np.concatenate([np.cos(ahead), -np.sin(ahead)], axis=0).T / block
    return [t.astype(np.float32).astype(ml_dtypes.bfloat16) for t in (forward, inverse)]


def kernel(
    gang,
    planes,
    scale,
    holder_ref,
    fwd_hbm,
    inv_hbm,
    x_ref,
    g_ref,
    taps_ref,
    o_ref,
    f_ref,
    fwd_ref,
    inv_ref,
    xbuf,
    gbuf,
    taps,
    xspec,
    gspec,
    fspec,
    prod,
    lag,
    outbuf,
    lag_send,
    lag_recv,
    lag_sum,
    local_sem,
    own_sem,
    x_send,
    x_recv,
    g_send,
    g_recv,
    gh_send,
    gh_recv,
    o_send,
    o_recv,
    f_send,
    f_recv,
    l_send,
    l_recv,
):
    me = lax.axis_index("ctx")
    q = me // gang
    j = me % gang
    halves, block, width = xbuf.shape[0], xbuf.shape[2], xbuf.shape[3]
    lag_block = f_ref.shape[0]
    half = block // 2

    def peer(d):
        found = 0
        bit = 1
        while bit < gang:
            found = found + ((j // bit + d // bit) % 2) * bit
            bit *= 2
        return found

    def cols(at, h):
        return pl.ds(pl.multiple_of((at * halves + h) * width, width), width)

    def remote(src, dst, send, recv, plane, at):
        return pltpu.make_async_remote_copy(
            src_ref=src,
            dst_ref=dst,
            send_sem=send,
            recv_sem=recv,
            device_id={"ctx": plane * gang + at},
            device_id_type=MESH,
        )

    barrier = pltpu.get_barrier_semaphore()
    for d in range(1, gang):
        pl.semaphore_signal(
            barrier, inc=1, device_id={"ctx": q * gang + peer(d)}, device_id_type=MESH
        )
    for e in range(1, planes):
        pl.semaphore_signal(
            barrier, inc=1, device_id={"ctx": ((q + e) % planes) * gang + j}, device_id_type=MESH
        )

    def own(n, h):
        source, target = [
            (x_ref.at[:, cols(j, h)], xbuf.at[h, j]),
            (g_ref.at[:, cols(j, h)], gbuf.at[h, 0, j]),
            (taps_ref.at[:, cols(j, h)], taps.at[h]),
        ][n]
        return pltpu.make_async_copy(source, target, own_sem.at[n, h])

    fetched = [
        pltpu.make_async_copy(fwd_hbm, fwd_ref, local_sem.at[0]),
        pltpu.make_async_copy(inv_hbm, inv_ref, local_sem.at[1]),
    ]
    fetched[0].start()
    for n in (2, 1, 0):
        for h in range(halves):
            own(n, h).start()
    fetched[1].start()

    pl.semaphore_wait(barrier, gang - 1 + planes - 1)

    def x_copy(h, d):
        return remote(
            x_ref.at[:, cols(peer(d), h)],
            xbuf.at[h, j],
            x_send.at[h, d],
            x_recv.at[h, d],
            q,
            peer(d),
        )

    def g_copy(h, d):
        return remote(
            g_ref.at[:, cols(peer(d), h)],
            gbuf.at[h, 0, j],
            g_send.at[h, d],
            g_recv.at[h, d],
            q,
            peer(d),
        )

    def g_ahead(h, d):
        source = g_ref.at[:, cols(j, h)] if d == 0 else gbuf.at[h, 0, peer(d)]
        return remote(
            source,
            gbuf.at[h, 1, peer(d)],
            gh_send.at[h, d],
            gh_recv.at[h, d],
            (q + planes - 1) % planes,
            j,
        )

    def arrived(ref, sem, at):
        remote(ref, ref, sem, sem, q, at).wait_recv()

    far_first = list(range(gang - 1, 0, -1))

    def send_g(h):
        for d in far_first:
            g_copy(h, d).start()

    def send_x(h):
        for d in far_first:
            x_copy(h, d).start()

    for h in range(halves):
        send_g(h)
    for h in range(halves):
        send_x(h)
    for h in range(halves):

        @pl.when(q > 0)
        def _():
            g_ahead(h, 0).start()

    @pl.when(q == planes - 1)
    def _():
        for h in range(halves):
            gbuf[h, 1] = jnp.zeros(gbuf.shape[2:], gbuf.dtype)

    def spectrum(value):
        return jnp.dot(fwd_ref[...], value, preferred_element_type=jnp.float32)

    fetched[0].wait()

    for h in range(halves):
        own(2, h).wait()

        @pl.loop(0, gang)
        def _(t):
            rows = pl.ds(pl.multiple_of(t * block, block), block)
            fspec[h, t] = spectrum(taps[h, rows, :].astype(jnp.bfloat16))

    def g_arrive(h):
        for d in range(1, gang):
            arrived(gbuf.at[h, 0, peer(d)], g_recv.at[h, d], peer(d))

            @pl.when(q > 0)
            def _():
                g_ahead(h, d).start()

    def x_arrive(h):
        for d in range(1, gang):
            arrived(xbuf.at[h, peer(d)], x_recv.at[h, d], peer(d))

    def g_spectra(h, side):
        @pl.loop(0, gang)
        def _(t):
            gspec[h, side * gang + t] = spectrum(gbuf[h, side, t])

    def x_spectra(h):
        @pl.loop(0, gang)
        def _(t):
            xspec[h, t] = spectrum(xbuf[h, t])

    def tiles(body):
        for part, sign in ((0, 1.0), (1, -1.0)):
            for lane in range(width // LANES):

                @pl.loop(0, half // ROWS)
                def _(step):
                    first = pl.multiple_of(part * half + step * ROWS, ROWS)
                    second = pl.multiple_of(block + part * half + step * ROWS, ROWS)
                    at = pl.ds(lane * LANES, LANES)
                    body(pl.ds(first, ROWS), pl.ds(second, ROWS), at, sign)

    def windows(h, real, imag, at, sign):
        parts = [(gspec[h, w, real, at], gspec[h, w, imag, at]) for w in range(2 * gang)]
        found = []
        for w in range(2 * gang - 1):
            low, high = parts[w], parts[w + 1]
            if sign > 0:
                found.append((low[0] + high[1], low[1] - high[0]))
            else:
                found.append((low[0] - high[1], low[1] + high[0]))
        return found

    def products(spec, h):
        def body(real, imag, at, sign):
            window = windows(h, real, imag, at, sign)
            lone = [(spec[h, t, real, at], spec[h, t, imag, at]) for t in range(gang)]
            for n in range(gang):
                total_r, total_i = None, None
                for t in range(gang):
                    a, b = lone[t], window[n + t]
                    r = a[0] * b[0] + a[1] * b[1]
                    i = a[0] * b[1] - a[1] * b[0]
                    total_r = r if total_r is None else total_r + r
                    total_i = i if total_i is None else total_i + i
                prod[n, real, at] = total_r.astype(jnp.bfloat16)
                prod[n, imag, at] = total_i.astype(jnp.bfloat16)

        tiles(body)

    def lag_copy(h, e):
        to = (q + e) % planes
        return remote(
            lag_send.at[h, to], lag_recv.at[h, q], l_send.at[h, e], l_recv.at[h, e], to, j
        )

    def lag_part(h):
        @pl.when(q < planes - 1)
        def _():
            for d in range(gang):
                arrived(gbuf.at[h, 1, peer(d)], gh_recv.at[h, d], j)

        g_spectra(h, 1)
        products(xspec, h)

        @pl.loop(0, gang)
        def _(o):
            found = jnp.dot(inv_ref[...], prod[o], preferred_element_type=jnp.float32)
            count = block // lag_block
            lag[pl.ds(o * count, count)] = found.reshape(count, lag_block, width)

        middle = planes // 2
        hops = sorted(range(1, planes), key=lambda e: abs(e - middle)) + [0]
        for e in range(planes):
            hop = hops[e]
            to = (q + hop) % planes
            pieces = []
            for at in range(gang):
                pieces.append(lag[holder_ref[to * gang + at]])
            whole = jnp.concatenate(pieces, axis=0)
            if e < planes - 1:
                lag_send[h, to] = whole.astype(jnp.bfloat16)
                lag_copy(h, hop).start()
            else:
                lag_sum[h] = whole

    def o_copy(h, d):
        return remote(
            outbuf.at[h, peer(d)],
            o_ref.at[:, cols(j, h)],
            o_send.at[h, d],
            o_recv.at[h, d],
            q,
            peer(d),
        )

    def own_o(h):
        return pltpu.make_async_copy(outbuf.at[h, j], o_ref.at[:, cols(j, h)], own_sem.at[3, h])

    def grad_part(h):
        products(fspec, h)

        @pl.loop(0, gang)
        def _(t):
            outbuf[h, t] = jnp.dot(
                inv_ref[...], prod[t], preferred_element_type=jnp.float32
            ).astype(jnp.bfloat16)

    def send_o(h):
        for d in far_first:
            o_copy(h, d).start()
        own_o(h).start()

    def lag_rows(h, at):
        return lag_sum.at[h, pl.ds(pl.multiple_of(at * lag_block, lag_block), lag_block), :]

    def f_copy(h, d):
        return remote(
            lag_rows(h, peer(d)),
            f_ref.at[:, cols(j, h)],
            f_send.at[h, d],
            f_recv.at[h, d],
            q,
            peer(d),
        )

    def own_f(h):
        return pltpu.make_async_copy(lag_rows(h, j), f_ref.at[:, cols(j, h)], own_sem.at[4, h])

    def lag_finish(h):
        total = lag_sum[h]
        for e in range(1, planes):
            source = (q + planes - e) % planes
            arrived(lag_recv.at[h, source], l_recv.at[h, e], j)
            total = total + lag_recv[h, source].astype(jnp.float32)
        lag_sum[h] = total * scale
        for d in far_first:
            f_copy(h, d).start()
        own_f(h).start()

    for h in range(halves):
        g_arrive(h)
    for h in range(halves):
        own(1, h).wait()
        g_spectra(h, 0)
        if h == 0:
            fetched[1].wait()
        else:
            grad_part(h - 1)
        x_arrive(h)
        own(0, h).wait()
        x_spectra(h)
        if h > 0:
            send_o(h - 1)
        lag_part(h)
    for h in range(halves - 1):
        lag_finish(h)
    grad_part(halves - 1)
    send_o(halves - 1)
    lag_finish(halves - 1)

    for h in range(halves):
        for d in range(1, gang):
            arrived(o_ref.at[:, cols(peer(d), h)], o_recv.at[h, d], peer(d))
            arrived(f_ref.at[:, cols(peer(d), h)], f_recv.at[h, d], peer(d))
            x_copy(h, d).wait_send()
            g_copy(h, d).wait_send()
            o_copy(h, d).wait_send()
            f_copy(h, d).wait_send()
        for e in range(1, planes):
            lag_copy(h, e).wait_send()

        @pl.when(q > 0)
        def _():
            for d in range(gang):
                g_ahead(h, d).wait_send()

        own_o(h).wait()
        own_f(h).wait()


def shards(inputs, out_grad, filter_taps, block_owner):
    block, channels = inputs.shape
    devices = lax.axis_size("ctx")
    lags = filter_taps.shape[0]
    gang = lags // block
    planes = devices // gang
    width = channels // gang // HALVES
    lag_block = lags // devices
    scale = 1.0 / math.sqrt(devices * block)
    ids = jnp.arange(devices, dtype=jnp.int32)
    holder = jnp.sum(
        jnp.where(block_owner[None, :] == ids[:, None], ids[None, :], 0), axis=1, dtype=jnp.int32
    )
    forward, inverse = [jnp.asarray(t) for t in make_tables(block)]
    hbm = pl.BlockSpec(memory_space=pltpu.HBM)
    dma = pltpu.SemaphoreType.DMA
    return pl.pallas_call(
        functools.partial(kernel, gang, planes, scale),
        out_shape=(
            jax.ShapeDtypeStruct((block, channels), jnp.bfloat16),
            jax.ShapeDtypeStruct((lag_block, channels), jnp.float32),
        ),
        in_specs=[pl.BlockSpec(memory_space=pltpu.SMEM)] + [hbm] * 5,
        out_specs=(hbm, hbm),
        scratch_shapes=[
            pltpu.VMEM(forward.shape, jnp.bfloat16),
            pltpu.VMEM(inverse.shape, jnp.bfloat16),
            pltpu.VMEM((HALVES, gang, block, width), jnp.bfloat16),
            pltpu.VMEM((HALVES, 2, gang, block, width), jnp.bfloat16),
            pltpu.VMEM((HALVES, lags, width), jnp.float32),
            pltpu.VMEM((HALVES, gang, 2 * block, width), jnp.float32),
            pltpu.VMEM((HALVES, 2 * gang, 2 * block, width), jnp.float32),
            pltpu.VMEM((HALVES, gang, 2 * block, width), jnp.float32),
            pltpu.VMEM((gang, 2 * block, width), jnp.bfloat16),
            pltpu.VMEM((devices, lag_block, width), jnp.float32),
            pltpu.VMEM((HALVES, gang, block, width), jnp.bfloat16),
            pltpu.VMEM((HALVES, planes, gang * lag_block, width), jnp.bfloat16),
            pltpu.VMEM((HALVES, planes, gang * lag_block, width), jnp.bfloat16),
            pltpu.VMEM((HALVES, gang * lag_block, width), jnp.float32),
            dma((2,)),
            dma((5, HALVES)),
        ]
        + [dma((HALVES, gang))] * 10
        + [dma((HALVES, planes))] * 2,
        compiler_params=pltpu.CompilerParams(
            collective_id=0, has_side_effects=True, vmem_limit_bytes=62 * 1024 * 1024
        ),
    )(holder, forward, inverse, inputs, out_grad, filter_taps)


def solution(mesh):
    placed = (P(("groups", "ctx"), None), P(("groups", "ctx"), None), P("groups", None), P())
    return jax.shard_map(
        shards,
        mesh=mesh,
        in_specs=placed,
        out_specs=(P(("groups", "ctx"), None), P(("groups", "ctx"), None)),
        check_vma=False,
    )
```
